256 devices in a mesh: section: 8 (over y, core), vocab: 8 (over z), dp: 4 (over x).
Axes of the slice: x: 4, y: 4, z: 8, core: 2. Of those that a mesh axis runs over, the one named last changes fastest.
Arguments:
- teacher_hidden: bfloat16 [640, 4096], P('dp', ('section', 'vocab')), as said below
- student_hidden: bfloat16 [640, 2048], P('dp', ('section', 'vocab')), as said below
- teacher_head: bfloat16 [4096, 65536], P('dp', ('section', 'vocab')), may hold values from -0.09375 to 0.09375
- student_head: bfloat16 [2048, 65536], P('dp', ('section', 'vocab')), may hold values from -0.125 to 0.125
- labels: int32 [640], P('dp'), may hold values from 0 to 65535
Outputs:
- loss: float32 [], replicated
- head_grad: float32 [2048, 65536], P('dp', ('section', 'vocab'))
- hidden_grad: bfloat16 [640, 2048], P('dp', ('section', 'vocab'))
The draws below stay inside these ranges and needn't reach their ends.
Inputs may be any that keep to these rules, and one draw needn't show every extreme that they name: `teacher_hidden`: Real-valued activations. `student_hidden`: Real-valued activations.
All inputs are finite; a program needn't handle non-finite values.
Results may differ from the reference program's by a relative error of at most 0.012.
Values may be sent and summed in bfloat16 or wider, within the bound.
A program may use at most 64 MiB of HBM per device.

```python
import math
import jax
import jax.numpy as jnp
import numpy as np

DT = 4096
DS = 2048
VOCAB = 65536
TOKENS = 640


def rough_rows(key, rows, cols, top, boost):
    first, second, third = jax.random.split(key, 3)
    scale = jnp.exp(jax.random.uniform(first, (rows, 1), minval=0.0, maxval=jnp.log(top)))
    values = jnp.clip(jax.random.normal(second, (rows, cols)), -5.0, 5.0)
    lifted = jnp.where(jax.random.randint(third, (rows, 1), 0, 16) == 0, boost, 1.0)
    return values * scale * lifted


def draw_teacher_hidden(key, part):
    key = jax.random.fold_in(key, 11)
    return rough_rows(key, TOKENS, DT, 10.0, 1.0).astype(jnp.bfloat16)


def draw_student_hidden(key, part):
    key = jax.random.fold_in(key, 12)
    return rough_rows(key, TOKENS, DS, 10.0, 1.0).astype(jnp.bfloat16)


def set_ends(drawn, rng, least, largest):
    longest = drawn.shape.index(max(drawn.shape))
    spots = []
    for shift in (0, 1):
        where = [jax.random.randint(jax.random.fold_in(rng, axis), (), 0, length) for axis, length in enumerate(drawn.shape)]
        where[longest] = (where[longest] + shift) % drawn.shape[longest]
        spots.append(tuple(where))
    return drawn.at[spots[0]].set(least).at[spots[1]].set(largest)


def levels(own_key, extent, pieces, smallest, high):
    level, own = 1.0, jax.random.fold_in(own_key, 6)
    for dim, shards_of in pieces:
        steps = jnp.exp(jax.random.uniform(jax.random.fold_in(own, dim), (shards_of,), jnp.float32, smallest / len(pieces), high / len(pieces)))
        level = level * jnp.repeat(steps, extent[dim] // shards_of).reshape([-1 if axis == dim else 1 for axis in range(len(extent))])
    return level


def rank_table(amount, skew):
    loads = [(1 << 20) // math.isqrt(standing ** skew) + 1 for standing in range(1, amount + 1)]
    deviation = 1 + sum(loads) // (1 << 30)
    return np.cumsum(np.array([max(1, weight // deviation) for weight in loads]))


def ranked_ids(rng, dims, amount, slope):
    table = rank_table(amount, slope)
    ticket = jax.random.randint(jax.random.fold_in(rng, 1), dims, 0, int(table[amount - 1]))
    grade = jnp.searchsorted(jnp.asarray(table, jnp.int32), ticket, side="right")
    return jax.random.permutation(jax.random.fold_in(rng, 2), amount)[grade].astype(jnp.int32)


def bell_draw(key, dims, spread, bound, cuts=(), kind=jnp.bfloat16):
    drawn = jax.random.normal(key, dims, jnp.float32) * spread
    if len(cuts) > 0:
        drawn = levels(key, dims, cuts, -0.22, 0.18) * drawn
    return jnp.clip(drawn, min=-bound, max=bound).astype(kind)


def setup_inputs(seed: int = 0) -> dict:
    key_list = jax.random.split(jax.random.key(seed), 6)
    teacher_hidden = draw_teacher_hidden(jax.random.fold_in(key_list[5], 71), 0)
    student_hidden = draw_student_hidden(jax.random.fold_in(key_list[5], 71), 0)
    teacher_head = bell_draw(key_list[2], (DT, VOCAB), DT ** -0.5, 0.09375, ((0, 4), (1, 64)))
    student_head = bell_draw(key_list[3], (DS, VOCAB), DS ** -0.5, 0.125, ((0, 4), (1, 64)))
    labels = set_ends(ranked_ids(key_list[4], (TOKENS,), VOCAB, 2), jax.random.fold_in(key_list[4], 3), 0, VOCAB - 1).astype(jnp.int32)
    return {"teacher_hidden": teacher_hidden, "student_hidden": student_hidden, "teacher_head": teacher_head, "student_head": student_head, "labels": labels}


label_weight = 0.5


def reference(teacher_hidden, student_hidden, teacher_head, student_head, labels):
    teacher_logits = jnp.dot(teacher_hidden, teacher_head, preferred_element_type=jnp.float32)
    student_logits = jnp.dot(student_hidden, student_head, preferred_element_type=jnp.float32)
    lt = jax.nn.log_softmax(teacher_logits, axis=-1)
    ls = jax.nn.log_softmax(student_logits, axis=-1)
    probs_t = jnp.exp(lt)
    probs_s = jnp.exp(ls)
    column = jnp.arange(VOCAB, dtype=jnp.int32)[None, :]
    onehot = (labels.astype(jnp.int32)[:, None] == column).astype(jnp.float32)
    per_token = jnp.sum(probs_t * (lt - ls), axis=-1) - label_weight * jnp.sum(onehot * ls, axis=-1)
    loss = jnp.sum(per_token) / TOKENS
    logit_grad = ((1.0 + label_weight) * probs_s - probs_t - label_weight * onehot).astype(jnp.bfloat16)
    head_grad = jnp.dot(student_hidden.T, logit_grad, preferred_element_type=jnp.float32)
    hidden_grad = jnp.dot(logit_grad, student_head.T, preferred_element_type=jnp.float32).astype(jnp.bfloat16)
    return loss, head_grad, hidden_grad
```

```python
import functools
import jax
import jax.numpy as jnp
from jax import lax
from jax.experimental import pallas as pl
from jax.experimental.pallas import tpu as pltpu
from jax.sharding import PartitionSpec as P

label_weight = 0.5
MESH = pl.DeviceIdType.MESH
F32, BF16, I32, I16 = jnp.float32, jnp.bfloat16, jnp.int32, jnp.int16
TOP = 14.99


def mm(a, b):
    return jnp.dot(a, b, preferred_element_type=F32)


def mm_nt(a, b):
    return lax.dot_general(a, b, (((1,), (1,)), ((), ())), preferred_element_type=F32)


def iota(shape, dim):
    return lax.broadcasted_iota(I32, shape, dim)


def ones_where(mask):
    return jnp.where(mask, 1.0, 0.0).astype(BF16)


def kernel(
    th, sh, wt_hbm, ws_hbm, lab,
    loss_out, hg, hid_out,
    wt, ws, packed, hslot, hid, hst, part, own_t, own_s,
    qsend, qrecv, grad, stat, stat_in, stat_mid, loss_in, cols_a, cols_b,
    hown, cbuf, crcv, zbuf, zrcv, ybuf, yrcv, fin, frcv,
    w_sem, h1_s, h1_r, zf_s, zf_r, zb_s, zb_r, cc_s, cc_r,
    q_s, q_r, st_s, st_r, sm_s, sm_r, lo_s, lo_r, g_s, g_r,
    c_s, c_r, z_s, z_r, y_s, y_r, f_s, f_r,
):
    tb = th.shape[0]
    half = tb // 2
    vb = wt.shape[1]
    ks = 128
    s = lax.axis_index("section")
    z = lax.axis_index("vocab")
    x = lax.axis_index("dp")
    y, c = lax.div(s, 2), lax.rem(s, 2)
    g4, j4 = lax.div(z, 4) * 4, lax.rem(z, 4)
    right, left, opp = lax.rem(x + 1, 4), lax.rem(x + 3, 4), lax.rem(x + 2, 4)
    mine = jnp.logical_and(x == y, j4 == x)
    pending = []

    def dev(section=s, vocab=z, dp=x):
        return {"section": section, "vocab": vocab, "dp": dp}

    def remote(src, dst, ssem, rsem, to):
        return pltpu.make_async_remote_copy(
            src_ref=src, dst_ref=dst, send_sem=ssem, recv_sem=rsem,
            device_id=to, device_id_type=MESH,
        )

    def send(src, dst, ssem, rsem, to):
        copy = remote(src, dst, ssem, rsem, to)
        copy.start()
        pending.append((None, copy))

    def send_if(cond, src, dst, ssem, rsem, to):
        copy = remote(src, dst, ssem, rsem, to)
        pl.when(cond)(copy.start)
        pending.append((cond, copy))

    def arrived(dst, ssem, rsem):
        remote(dst, dst, ssem, rsem, dev(dp=right)).wait_recv()

    load_t = pltpu.make_async_copy(wt_hbm, wt, w_sem.at[0])
    load_s = pltpu.make_async_copy(ws_hbm, ws, w_sem.at[1])
    load_t.start()
    load_s.start()

    barrier = pltpu.get_barrier_semaphore()

    def greet(to):
        pl.semaphore_signal(barrier, inc=1, device_id=to, device_id_type=MESH)

    for k in range(1, 4):
        greet(dev(dp=lax.rem(x + k, 4)))
    for k in range(1, 8):
        greet(dev(vocab=lax.rem(z + k, 8)))
        greet(dev(section=lax.rem(s + k, 8)))
    for k in range(4):
        to = dev(section=2 * k + c, vocab=g4 + x, dp=y)
        pl.when(jnp.logical_not(jnp.logical_and(mine, y == k)))(functools.partial(greet, to))
        frm = dev(section=2 * x + c, vocab=g4 + k, dp=j4)
        pl.when(jnp.logical_not(jnp.logical_and(mine, j4 == k)))(functools.partial(greet, frm))

    packed[...] = (
        mm(th[...], ones_where(iota((64, 128), 0) == iota((64, 128), 1)))
        + mm(sh[...], ones_where(iota((32, 128), 0) + 64 == iota((32, 128), 1)))
    ).astype(BF16)
    pl.semaphore_wait(barrier, 25 - 2 * mine.astype(I32))

    for k in range(4):
        send_if(
            jnp.logical_not(jnp.logical_and(mine, y == k)),
            packed, hslot.at[j4], h1_s.at[k], h1_r.at[j4],
            dev(section=2 * k + c, vocab=g4 + x, dp=y),
        )

    @pl.when(mine)
    def _():
        hslot[j4] = packed[...]

    cols_b[...] = jnp.zeros_like(cols_b)
    cols_b[0:1, 0:tb] = lab[...].astype(F32)
    lab_cols = cols_b[...].T
    cols_a[...] = lab_cols
    stat[...] = jnp.ones_like(stat)

    unit = None
    for k in range(4):
        @pl.when(jnp.logical_not(jnp.logical_and(mine, j4 == k)))
        def _(k=k):
            arrived(hslot.at[k], h1_s.at[k], h1_r.at[k])

    for k in range(4):
        rows, lanes = iota((128, 384), 0), iota((128, 384), 1)
        place = jnp.where(rows < 64, rows + 64 * k, rows - 64 + 256 + 32 * k)
        pick = ones_where(jnp.logical_and(lanes == place, rows < 96))
        term = mm(hslot[k], pick)
        unit = term if unit is None else unit + term
    hid[c, z] = unit.astype(BF16)

    sgn = 1 - 2 * c
    ahead, behind = lax.rem(z + sgn + 8, 8), lax.rem(z - sgn + 8, 8)
    other = dev(section=s + sgn)

    def rows_of(h):
        return pl.ds(h * half, half)

    def block(k):
        return lax.rem(z + k * sgn + 16, 8)

    def to_ahead(k, h):
        b = block(1 - k)
        ref = hid.at[c, b, rows_of(h)]
        send(ref, ref, zf_s.at[2 * k - 2 + h], zf_r.at[2 * k - 2 + h], dev(vocab=ahead))

    def to_behind(k, h):
        b = block(k - 1)
        ref = hid.at[c, b, rows_of(h)]
        send(ref, ref, zb_s.at[2 * k - 2 + h], zb_r.at[2 * k - 2 + h], dev(vocab=behind))

    def to_other(b, h):
        ref = hid.at[c, b, rows_of(h)]
        send(ref, ref, cc_s.at[2 * b + h], cc_r.at[2 * b + h], other)

    for h in range(2):
        to_ahead(1, h)
        to_behind(1, h)
    for h in range(2):
        to_other(z, h)
    for k in range(1, 5):
        for h in range(2):
            b = block(-k)
            arrived(hid.at[c, b, rows_of(h)], zf_s.at[2 * k - 2 + h], zf_r.at[2 * k - 2 + h])
            if k < 4:
                to_ahead(k + 1, h)
            to_other(b, h)
            if k < 4:
                b = block(k)
                arrived(hid.at[c, b, rows_of(h)], zb_s.at[2 * k - 2 + h], zb_r.at[2 * k - 2 + h])
                if k < 3:
                    to_behind(k + 1, h)
                to_other(b, h)
    load_t.wait()
    load_s.wait()
    for b in range(8):
        for h in range(2):
            arrived(hid.at[1 - c, b, rows_of(h)], cc_s.at[2 * b + h], cc_r.at[2 * b + h])

    def logits_t(xp, out):
        def body(n, carry):
            cols = pl.ds(pl.multiple_of(n * 256, 256), 256)
            total = None
            for u in range(4):
                term = mm(hid[u // 2, 4 * (u % 2) + xp, :, 0:256], wt[u * 256:(u + 1) * 256, cols])
                total = term if total is None else total + term
            out[:, cols] = total
            return carry
        lax.fori_loop(0, vb // 256, body, 0)

    def logits_s(xp, out):
        def body(n, carry):
            cols = pl.ds(pl.multiple_of(n * 256, 256), 256)
            total = None
            for u in range(4):
                term = mm(hid[u // 2, 4 * (u % 2) + xp, :, 256:384], ws[u * ks:(u + 1) * ks, cols])
                total = term if total is None else total + term
            out[:, cols] = total
            return carry
        lax.fori_loop(0, vb // 256, body, 0)

    def decode(slot, rows):
        step = jnp.exp2(qrecv[slot, rows, vb:vb + 128].astype(F32) * 0.25 - TOP)
        return jnp.concatenate(
            [qrecv[slot, rows, i:i + 128].astype(F32) * step for i in range(0, vb, 128)], axis=1
        )

    def encode(slot, src, add=None):
        def body(r, carry):
            rows = pl.ds(pl.multiple_of(r * 16, 16), 16)
            v = src[rows, :]
            if add is not None:
                v = v + decode(add, rows)
            top = jnp.maximum(jnp.max(jnp.abs(v), axis=1, keepdims=True), 1e-30)
            level = jnp.broadcast_to(jnp.ceil(jnp.log2(top) * 4.0), (16, 128))
            scale = jnp.exp2(TOP - level * 0.25)
            for i in range(0, vb, 128):
                q = jnp.round(v[:, i:i + 128] * scale).astype(I32)
                qsend[slot, rows, i:i + 128] = q.astype(I16)
            qsend[slot, rows, vb:vb + 128] = level.astype(I32).astype(I16)
            return carry
        lax.fori_loop(0, tb // 16, body, 0)

    def ship(slot, dp):
        send(qsend.at[slot], qrecv.at[slot], q_s.at[slot], q_r.at[slot], dev(dp=dp))

    def landed(slot):
        arrived(qrecv.at[slot], q_s.at[slot], q_r.at[slot])

    logits_t(opp, part)
    encode(0, part)
    ship(0, right)
    logits_s(opp, part)
    encode(3, part)
    ship(3, left)
    logits_s(right, part)
    encode(1, part)
    ship(1, right)
    logits_t(left, part)
    encode(4, part)
    ship(4, left)
    logits_t(right, own_t)
    logits_s(left, own_s)
    landed(0)
    encode(2, own_t, add=0)
    ship(2, right)
    landed(3)
    encode(5, own_s, add=3)
    ship(5, left)
    logits_t(x, own_t)
    logits_s(x, own_s)

    eye = ones_where(iota((128, 128), 0) == iota((128, 128), 1))
    for u in range(4):
        def turn(xp, carry, u=u):
            flat = mm_nt(eye, hid[u // 2, 4 * (u % 2) + xp, :, 256:384])
            hst[xp, u * 128:(u + 1) * 128, :] = flat.astype(BF16)
            return carry
        lax.fori_loop(0, 4, turn, 0)

    landed(1)
    landed(4)
    landed(2)
    landed(5)

    offset = (s * 8 + z) * vb

    def collect(r, carry):
        rows = pl.ds(pl.multiple_of(r * 16, 16), 16)
        lt = own_t[rows, :] + decode(4, rows) + decode(2, rows)
        ls = own_s[rows, :] + decode(1, rows) + decode(5, rows)
        own_t[rows, :] = lt
        own_s[rows, :] = ls
        mt = jnp.max(lt, axis=1, keepdims=True)
        ms = jnp.max(ls, axis=1, keepdims=True)
        et = jnp.exp(lt - mt)
        es = jnp.exp(ls - ms)
        column = offset + iota((16, vb), 1)
        hit = column == cols_a[rows, 0:1].astype(I32)
        values = (
            mt,
            jnp.sum(et, axis=1, keepdims=True),
            jnp.sum(et * (lt - ls), axis=1, keepdims=True),
            ms,
            jnp.sum(es, axis=1, keepdims=True),
            jnp.sum(jnp.where(hit, ls, 0.0), axis=1, keepdims=True),
        )
        lane = iota((16, 128), 1)
        out = jnp.ones((16, 128), F32)
        for i, value in enumerate(values):
            out = jnp.where(lane == i, value, out)
        stat[rows, :] = out
        return carry

    lax.fori_loop(0, tb // 16, collect, 0)

    def merge(ref):
        tops_t = [ref[i, 0:1, :] for i in range(8)]
        tops_s = [ref[i, 3:4, :] for i in range(8)]
        mt = functools.reduce(jnp.maximum, tops_t)
        ms = functools.reduce(jnp.maximum, tops_s)
        zt = at = zs = sy = 0.0
        for i in range(8):
            wt_i = jnp.exp(tops_t[i] - mt)
            ws_i = jnp.exp(tops_s[i] - ms)
            zt = zt + ref[i, 1:2, :] * wt_i
            at = at + ref[i, 2:3, :] * wt_i
            zs = zs + ref[i, 4:5, :] * ws_i
            sy = sy + ref[i, 5:6, :]
        return mt, zt, at, ms, zs, sy

    turned = stat[...].T
    stat_in[z] = turned[0:8, :]
    for k in range(1, 8):
        send(stat_in.at[z], stat_in.at[z], st_s.at[k], st_r.at[z], dev(vocab=lax.rem(z + k, 8)))
    for k in range(1, 8):
        frm = lax.rem(z + k, 8)
        arrived(stat_in.at[frm], st_s.at[k], st_r.at[frm])
    pieces = merge(stat_in)
    for i, piece in enumerate(pieces):
        stat_mid[s, i:i + 1, :] = piece
    for k in range(1, 8):
        send(stat_mid.at[s], stat_mid.at[s], sm_s.at[k], sm_r.at[s], dev(section=lax.rem(s + k, 8)))
    for k in range(1, 8):
        frm = lax.rem(s + k, 8)
        arrived(stat_mid.at[frm], sm_s.at[k], sm_r.at[frm])
    mt, zt, at, ms, zs, sy = merge(stat_mid)
    lse_t = mt + jnp.log(zt)
    lse_s = ms + jnp.log(zs)
    per_token = at / zt - lse_t + lse_s - label_weight * (sy - lse_s)
    per_token = jnp.where(iota((1, 256), 1) < tb, per_token, 0.0)
    cols_b[0:1, :] = lse_t
    cols_b[1:2, :] = lse_s
    turned = cols_b[...].T
    stat[...] = turned

    def finish(r, carry):
        rows = pl.ds(pl.multiple_of(r * 16, 16), 16)
        column = offset + iota((16, vb), 1)
        hit = column == cols_a[rows, 0:1].astype(I32)
        pt = jnp.exp(own_t[rows, :] - stat[rows, 0:1])
        ps = jnp.exp(own_s[rows, :] - stat[rows, 1:2])
        value = (1.0 + label_weight) * ps - pt - jnp.where(hit, label_weight, 0.0)
        grad[x, rows, :] = value.astype(BF16)
        return carry

    def gsend(owner, h, i, dp):
        ref = grad.at[owner, rows_of(h)]
        send(ref, ref, g_s.at[i], g_r.at[i], dev(dp=dp))

    def gwait(owner, h, i):
        arrived(grad.at[owner, rows_of(h)], g_s.at[i], g_r.at[i])

    lax.fori_loop(0, half // 16, finish, 0)
    gsend(x, 0, 0, right)
    gsend(x, 0, 3, left)
    lax.fori_loop(half // 16, tb // 16, finish, 0)
    gsend(x, 1, 2, left)
    gsend(x, 1, 1, right)
    loss_in[x] = jnp.broadcast_to(jnp.sum(per_token, axis=1, keepdims=True), (8, 128))
    for k in range(1, 4):
        send(loss_in.at[x], loss_in.at[x], lo_s.at[k], lo_r.at[x], dev(dp=lax.rem(x + k, 4)))

    def hidden_terms(xp):
        for g in range(2):
            u = (1 - c) * 2 + g
            rows = pl.ds(pl.multiple_of(u * ks, ks), ks)
            cbuf[xp, g] = mm_nt(grad[xp], ws[rows, :]).astype(BF16)
        send(cbuf.at[xp], crcv.at[xp], c_s.at[xp], c_r.at[xp], other)
        for g in range(2):
            u = c * 2 + g
            rows = pl.ds(pl.multiple_of(u * ks, ks), ks)
            hown[xp, g] = mm_nt(grad[xp], ws[rows, :])

    def head_terms(xp, first):
        def body(n, carry):
            cols = pl.ds(pl.multiple_of(n * 256, 256), 256)
            term = mm(hst[xp], grad[xp, :, cols])
            hg[:, cols] = term if first else hg[:, cols] + term
            return carry
        lax.fori_loop(0, vb // 256, body, 0)

    def spread(xp):
        arrived(crcv.at[xp], c_s.at[xp], c_r.at[xp])
        for g in range(2):
            total = hown[xp, g] + crcv[xp, g].astype(F32)
            hown[xp, g] = total
            zbuf[xp, g] = total.astype(BF16)
            to = 4 * g + xp
            send_if(to != z, zbuf.at[xp, g], zrcv.at[z], z_s.at[2 * xp + g], z_r.at[z], dev(vocab=to))

    hidden_terms(x)
    head_terms(x, True)
    spread(x)
    gwait(left, 0, 0)
    gsend(left, 0, 4, right)
    gwait(right, 1, 2)
    gsend(right, 1, 5, left)
    gwait(left, 1, 1)
    hidden_terms(left)
    head_terms(left, False)
    spread(left)
    gwait(right, 0, 3)
    hidden_terms(right)
    head_terms(right, False)
    spread(right)
    gwait(opp, 0, 4)
    gwait(opp, 1, 5)
    hidden_terms(opp)
    head_terms(opp, False)
    spread(opp)

    total = hown[j4, lax.div(z, 4)]
    for k in range(1, 8):
        frm = lax.rem(z + k, 8)
        arrived(zrcv.at[frm], z_s.at[k], z_r.at[frm])
        total = total + zrcv[frm].astype(F32)
    ybuf[...] = total.astype(BF16)
    send_if(x != y, ybuf, yrcv.at[y], y_s, y_r.at[y], dev(section=2 * x + c))
    hown[j4, lax.div(z, 4)] = total

    @pl.when(x == y)
    def _():
        whole = hown[j4, lax.div(z, 4)]
        for k in range(1, 4):
            frm = lax.rem(y + k, 4)
            arrived(yrcv.at[frm], y_s, y_r.at[frm])
            whole = whole + yrcv[frm].astype(F32)
        fin[...] = whole.astype(BF16)

    for k in range(4):
        there = jnp.logical_and(j4 == x, j4 == k)
        send_if(
            jnp.logical_and(x == y, jnp.logical_not(there)),
            fin, frcv, f_s.at[k], f_r, dev(vocab=g4 + k, dp=j4),
        )

    @pl.when(mine)
    def _():
        frcv[...] = fin[...]

    @pl.when(jnp.logical_not(mine))
    def _():
        arrived(frcv, f_s.at[0], f_r)

    pick = ones_where(iota((128, 32), 0) == iota((128, 32), 1) + 32 * j4)
    hid_out[...] = mm(frcv[...], pick).astype(BF16)

    loss = loss_in[x, 0:1, 0:1]
    for k in range(1, 4):
        frm = lax.rem(x + k, 4)
        arrived(loss_in.at[frm], lo_s.at[k], lo_r.at[frm])
    loss = loss_in[0, 0:1, 0:1] + loss_in[1, 0:1, 0:1] + loss_in[2, 0:1, 0:1] + loss_in[3, 0:1, 0:1]
    loss_out[0, 0] = jnp.sum(loss) / (4.0 * tb)

    for cond, copy in pending:
        if cond is None:
            copy.wait_send()
        else:
            pl.when(cond)(copy.wait_send)


def per_device(teacher_hidden, student_hidden, teacher_head, student_head, labels):
    tb = teacher_hidden.shape[0]
    kt, vb = teacher_head.shape
    ks = student_head.shape[0]
    dma, vmem = pltpu.SemaphoreType.DMA, pltpu.VMEM
    loss, head_grad, hidden_grad = pl.pallas_call(
        kernel,
        out_shape=(
            jax.ShapeDtypeStruct((1, 1), F32),
            jax.ShapeDtypeStruct((ks, vb), F32),
            jax.ShapeDtypeStruct((tb, 32), BF16),
        ),
        in_specs=[
            pl.BlockSpec(memory_space=pltpu.VMEM),
            pl.BlockSpec(memory_space=pltpu.VMEM),
            pl.BlockSpec(memory_space=pl.ANY),
            pl.BlockSpec(memory_space=pl.ANY),
            pl.BlockSpec(memory_space=pltpu.VMEM),
        ],
        out_specs=(
            pl.BlockSpec(memory_space=pltpu.SMEM),
            pl.BlockSpec(memory_space=pltpu.VMEM),
            pl.BlockSpec(memory_space=pltpu.VMEM),
        ),
        scratch_shapes=[
            vmem((kt, vb), BF16),
            vmem((ks, vb), BF16),
            vmem((tb, 128), BF16),
            vmem((4, tb, 128), BF16),
            vmem((2, 8, tb, 384), BF16),
            vmem((4, ks, tb), BF16),
            vmem((tb, vb), F32),
            vmem((tb, vb), F32),
            vmem((tb, vb), F32),
            vmem((6, tb, vb + 128), I16),
            vmem((6, tb, vb + 128), I16),
            vmem((4, tb, vb), BF16),
            vmem((256, 128), F32),
            vmem((8, 8, 256), F32),
            vmem((8, 8, 256), F32),
            vmem((4, 8, 128), F32),
            vmem((256, 128), F32),
            vmem((128, 256), F32),
            vmem((4, 2, tb, 128), F32),
            vmem((4, 2, tb, 128), BF16),
            vmem((4, 2, tb, 128), BF16),
            vmem((4, 2, tb, 128), BF16),
            vmem((8, tb, 128), BF16),
            vmem((tb, 128), BF16),
            vmem((4, tb, 128), BF16),
            vmem((tb, 128), BF16),
            vmem((tb, 128), BF16),
            dma((2,)), dma((4,)), dma((4,)),
            dma((8,)), dma((8,)), dma((6,)), dma((6,)), dma((16,)), dma((16,)),
            dma((6,)), dma((6,)), dma((8,)), dma((8,)), dma((8,)), dma((8,)),
            dma((4,)), dma((4,)), dma((6,)), dma((6,)),
            dma((4,)), dma((4,)), dma((8,)), dma((8,)),
            dma, dma((4,)), dma((4,)), dma,
        ],
        compiler_params=pltpu.CompilerParams(
            collective_id=0, has_side_effects=True, vmem_limit_bytes=48 * 1024 * 1024
        ),
    )(teacher_hidden, student_hidden, teacher_head, student_head, labels.reshape(1, tb))
    return (loss.reshape(()), head_grad, hidden_grad)


def solution(mesh):
    spec = P("dp", ("section", "vocab"))
    return jax.shard_map(
        per_device,
        mesh=mesh,
        in_specs=(spec, spec, spec, spec, P("dp")),
        out_specs=(P(), spec, spec),
        check_vma=False,
    )
```

```python
import functools
import jax
import jax.numpy as jnp
from jax import lax
from jax.experimental import pallas as pl
from jax.experimental.pallas import tpu as pltpu
from jax.sharding import PartitionSpec as P

label_weight = 0.5
MESH = pl.DeviceIdType.MESH
F32, BF16, I32, I16 = jnp.float32, jnp.bfloat16, jnp.int32, jnp.int16
TOP = 14.99
PARTS = (48, 64, 48)
ORDER = (
    "F2", "F1", "I", "Z2", "F0", "Z1", "Y2", "Y1", "W2", "Z0", "L2", "W1", "Y0", "U2",
    "O2", "L1", "T2", "W0", "O1", "L0", "U1", "T1", "S2", "O0", "S1", "G2", "T0", "G1",
    "U0", "S0", "B2", "G0", "P2", "B1", "P1", "B0", "P0", "N1", "X", "N2", "H", "X2",
    "N0", "E",
)


def mm(a, b):
    return jnp.dot(a, b, preferred_element_type=F32)


def mm_nt(a, b):
    return lax.dot_general(a, b, (((1,), (1,)), ((), ())), preferred_element_type=F32)


def iota(shape, dim):
    return lax.broadcasted_iota(I32, shape, dim)


def ones_where(mask):
    return jnp.where(mask, 1.0, 0.0).astype(BF16)


def buffers(tb, kt, ks, vb):
    dma, vmem = pltpu.SemaphoreType.DMA, pltpu.VMEM

    def each(make):
        return [make(n) for n in PARTS]

    return {
        "wt": vmem((kt, vb), BF16),
        "ws": vmem((ks, vb), BF16),
        "lab": vmem((1, tb), I32),
        "turned": vmem((128, tb), BF16),
        "packed": vmem((tb, 128), BF16),
        "wide": vmem((128, 256), F32),
        "lab_col": vmem((256, 128), F32),
        "raw": each(lambda n: vmem((8, n, 128), BF16)),
        "hid": each(lambda n: vmem((2, 4 * n, 768), BF16)),
        "hst": each(lambda n: vmem((ks, 4 * n), BF16)),
        "part_t": each(lambda n: vmem((4 * n, vb), F32)),
        "part_s": each(lambda n: vmem((4 * n, vb), F32)),
        "qsend": each(lambda n: vmem((6, n, vb + 128), I16)),
        "qrecv": each(lambda n: vmem((6, n, vb + 128), I16)),
        "level": each(lambda n: vmem((2, n, 128), F32)),
        "stat": each(lambda n: vmem((128, 128), F32)),
        "lse": each(lambda n: vmem((128, 128), F32)),
        "stat_z": each(lambda n: vmem((8, 8, 128), F32)),
        "stat_s": each(lambda n: vmem((8, 8, 128), F32)),
        "grad": each(lambda n: vmem((4 * n, vb), BF16)),
        "hown": each(lambda n: vmem((256, 4 * n), F32)),
        "csend": each(lambda n: vmem((256, 4 * n), BF16)),
        "crecv": each(lambda n: vmem((256, 4 * n), BF16)),
        "zsend": each(lambda n: vmem((256, 4 * n), BF16)),
        "zrecv": each(lambda n: vmem((8, 32, 4 * n), BF16)),
        "fsend": each(lambda n: vmem((32, 4 * n), BF16)),
        "frecv": each(lambda n: vmem((4, 32, 4 * n), BF16)),
        "loss": vmem((4, 8, 128), F32),
        "in_sem": dma((5,)),
        "h_s": each(lambda n: dma),
        "h_r": each(lambda n: dma),
        "r_s": each(lambda n: dma((8,))),
        "r_r": each(lambda n: dma((8,))),
        "u_s": each(lambda n: dma((4,))),
        "u_r": each(lambda n: dma((4,))),
        "w_s": each(lambda n: dma((4,))),
        "w_r": each(lambda n: dma((4,))),
        "q_s": each(lambda n: dma((6,))),
        "q_r": each(lambda n: dma((6,))),
        "sz_s": each(lambda n: dma((8,))),
        "sz_r": each(lambda n: dma((8,))),
        "ss_s": each(lambda n: dma((8,))),
        "ss_r": each(lambda n: dma((8,))),
        "g_s": each(lambda n: dma((4,))),
        "g_r": each(lambda n: dma((4,))),
        "c_s": each(lambda n: dma),
        "c_r": each(lambda n: dma),
        "z_s": each(lambda n: dma((8,))),
        "z_r": each(lambda n: dma((8,))),
        "f_s": each(lambda n: dma((4,))),
        "f_r": each(lambda n: dma((4,))),
        "l_s": dma((4,)),
        "l_r": dma((4,)),
    }


class Refs:
    pass


def kernel(spec, th, sh, wt_hbm, ws_hbm, lab_hbm, loss_out, hg, hid_out, *scratch):
    m = Refs()
    scratch = list(scratch)
    for name, shape in spec.items():
        if isinstance(shape, list):
            setattr(m, name, [scratch.pop(0) for _ in shape])
        else:
            setattr(m, name, scratch.pop(0))
    tb = m.packed.shape[0]
    vb = m.wt.shape[1]
    s = lax.axis_index("section")
    z = lax.axis_index("vocab")
    x = lax.axis_index("dp")
    y, c = lax.div(s, 2), lax.rem(s, 2)
    right, left, opp = lax.rem(x + 1, 4), lax.rem(x + 3, 4), lax.rem(x + 2, 4)
    diagonal = x == y
    crossed = jnp.logical_not(diagonal)
    offset = (s * 8 + z) * vb
    starts = [sum(PARTS[:k]) for k in range(len(PARTS))]
    pending = []

    def dev(section=s, vocab=z, dp=x):
        return {"section": section, "vocab": vocab, "dp": dp}

    def remote(src, dst, ssem, rsem, to):
        return pltpu.make_async_remote_copy(
            src_ref=src, dst_ref=dst, send_sem=ssem, recv_sem=rsem,
            device_id=to, device_id_type=MESH,
        )

    def send(src, dst, ssem, rsem, to, cond=None):
        copy = remote(src, dst, ssem, rsem, to)
        if cond is None:
            copy.start()
        else:
            pl.when(cond)(copy.start)
        pending.append((cond, copy))

    def arrived(dst, ssem, rsem):
        remote(dst, dst, ssem, rsem, dev(dp=right)).wait_recv()

    other = dev(section=s + 1 - 2 * c)

    local = [
        pltpu.make_async_copy(th, m.turned.at[0:64], m.in_sem.at[0]),
        pltpu.make_async_copy(sh, m.turned.at[64:96], m.in_sem.at[1]),
        pltpu.make_async_copy(lab_hbm, m.lab, m.in_sem.at[2]),
        pltpu.make_async_copy(wt_hbm, m.wt, m.in_sem.at[3]),
        pltpu.make_async_copy(ws_hbm, m.ws, m.in_sem.at[4]),
    ]
    for copy in local:
        copy.start()

    barrier = pltpu.get_barrier_semaphore()

    def greet(to, unless=None):
        signal = functools.partial(
            pl.semaphore_signal, barrier, inc=1, device_id=to, device_id_type=MESH
        )
        if unless is None:
            signal()
        else:
            pl.when(jnp.logical_not(unless))(signal)

    def last_to(k):
        return dev(section=2 * x + c, dp=k), jnp.logical_and(diagonal, x == k)

    for k in range(1, 8):
        greet(dev(vocab=lax.rem(z + k, 8)))
    for k in range(1, 4):
        greet(dev(section=2 * x + c, dp=lax.rem(x + k, 4)))
    for k in range(4):
        greet(dev(section=2 * k + c, dp=y), diagonal)
    for k in range(1, 4):
        greet(dev(dp=lax.rem(x + k, 4)))
    for k in range(1, 8):
        greet(dev(section=lax.rem(s + k, 8)))

    for copy in local[:3]:
        copy.wait()
    m.turned[96:128, :] = jnp.zeros((32, tb), BF16)
    m.packed[...] = mm_nt(
        ones_where(iota((tb, tb), 0) == iota((tb, tb), 1)), m.turned[...]
    ).astype(BF16)
    pl.semaphore_wait(barrier, 20 + 4 * crossed.astype(I32))

    def hidden_first(p):
        rows = pl.ds(starts[p], PARTS[p])
        send(m.packed.at[rows], m.raw[p].at[z], m.h_s[p], m.h_r[p], dev(section=2 * x + c, dp=y), crossed)

        @pl.when(diagonal)
        def _():
            m.raw[p][z] = m.packed[rows, :]

    def hidden_z(p):
        ref = m.raw[p].at[z]

        @pl.when(crossed)
        def _():
            arrived(ref, m.h_s[p], m.h_r[p])

        for k in (4, 3, 5, 2, 6, 1, 7):
            send(ref, ref, m.r_s[p].at[k], m.r_r[p].at[z], dev(vocab=lax.rem(z + k, 8)))

    picks = []

    def hid_ref(p, core, yy):
        n = PARTS[p]
        return m.hid[p].at[core, pl.ds(pl.multiple_of(yy * n, n), n)]

    def hidden_y(p):
        for k in (1, 7, 2, 6, 3, 5, 4):
            frm = lax.rem(z + k, 8)
            arrived(m.raw[p].at[frm], m.r_s[p].at[k], m.r_r[p].at[frm])
        ref = hid_ref(p, c, y)
        for g in range(2):
            total = None
            for k in range(4):
                term = mm(m.raw[p][4 * g + k], picks[k])
                total = term if total is None else total + term
            ref[:, g * 256:(g + 1) * 256] = total[:, 0:256].astype(BF16)
            ref[:, 512 + g * 128:512 + (g + 1) * 128] = total[:, 256:384].astype(BF16)
        for k in (2, 1, 3):
            to = lax.rem(y + k, 4)
            send(ref, ref, m.u_s[p].at[k], m.u_r[p].at[y], dev(section=2 * to + c))
        send(ref, ref, m.w_s[p].at[y], m.w_r[p].at[y], other)

    def hidden_swap(p):
        for k in (1, 3, 2):
            frm = lax.rem(y + k, 4)
            ref = hid_ref(p, c, frm)
            arrived(ref, m.u_s[p].at[k], m.u_r[p].at[frm])
            send(ref, ref, m.w_s[p].at[frm], m.w_r[p].at[frm], other)

    def decode(p, slot, rows):
        if slot in (1, 4):
            level = m.qrecv[p][slot + 1, rows, vb:vb + 128][:, 64:65]
        else:
            level = m.qrecv[p][slot, rows, vb:vb + 128][:, 0:1]
        step = jnp.exp2(jnp.broadcast_to(level.astype(F32), (16, 128)) * 0.25 - TOP)
        return jnp.concatenate(
            [m.qrecv[p][slot, rows, i:i + 128].astype(F32) * step for i in range(0, vb, 128)],
            axis=1,
        )

    def word_refs(p, slot):
        lanes = slice(0, vb if slot in (1, 4) else vb + 128)
        return m.qsend[p].at[slot, :, lanes], m.qrecv[p].at[slot, :, lanes]

    def encode(p, slot, src, xp, dp, add=None):
        n = PARTS[p]

        def body(r, carry):
            rows = pl.ds(pl.multiple_of(r * 16, 16), 16)
            v = src[pl.ds(pl.multiple_of(xp * n + r * 16, 16), 16), :]
            if add is not None:
                v = v + decode(p, add, rows)
            top = jnp.maximum(jnp.max(jnp.abs(v), axis=1, keepdims=True), 1e-30)
            level = jnp.broadcast_to(jnp.ceil(jnp.log2(top) * 4.0), (16, 128))
            scale = jnp.exp2(TOP - level * 0.25)
            for i in range(0, vb, 128):
                q = jnp.round(v[:, i:i + 128] * scale).astype(I32)
                m.qsend[p][slot, rows, i:i + 128] = q.astype(I16)
            if slot in (1, 4):
                m.level[p][slot // 4, rows, :] = level
            else:
                if slot in (2, 5):
                    beside = m.level[p][slot // 5, rows, :]
                    level = jnp.where(iota((16, 128), 1) < 64, level, beside)
                m.qsend[p][slot, rows, vb:vb + 128] = level.astype(I32).astype(I16)
            return carry

        lax.fori_loop(0, n // 16, body, 0, unroll=True)
        src_words, dst_words = word_refs(p, slot)
        send(src_words, dst_words, m.q_s[p].at[slot], m.q_r[p].at[slot], dev(dp=dp))

    def landed(p, slot):
        arrived(word_refs(p, slot)[1], m.q_s[p].at[slot], m.q_r[p].at[slot])

    def logits(p):
        for k in range(4):
            arrived(hid_ref(p, 1 - c, k), m.w_s[p].at[k], m.w_r[p].at[k])

        def product(out, weights, lanes, depth):
            def body(i, carry):
                cols = pl.ds(pl.multiple_of(i * 256, 256), 256)
                out[:, cols] = mm(m.hid[p][0, :, lanes], weights[0:depth, cols]) + mm(
                    m.hid[p][1, :, lanes], weights[depth:2 * depth, cols]
                )
                return carry
            lax.fori_loop(0, vb // 256, body, 0)

        product(m.part_t[p], m.wt, slice(0, 512), 512)
        encode(p, 0, m.part_t[p], opp, right)
        product(m.part_s[p], m.ws, slice(512, 768), 256)
        encode(p, 3, m.part_s[p], opp, left)
        encode(p, 1, m.part_s[p], right, right)
        encode(p, 4, m.part_t[p], left, left)

    def fold(p):
        landed(p, 0)
        encode(p, 2, m.part_t[p], right, right, add=0)
        landed(p, 3)
        encode(p, 5, m.part_s[p], left, left, add=3)

    def row_span(p, r):
        n = PARTS[p]
        rows = pl.ds(pl.multiple_of(r * 16, 16), 16)
        own = pl.ds(pl.multiple_of(x * n + r * 16, 16), 16)
        toks = pl.ds(pl.multiple_of(starts[p] + r * 16, 16), 16)
        hit = offset + iota((16, vb), 1) == m.lab_col[toks, 0:1].astype(I32)
        return rows, own, hit

    def total_logits(p):
        for slot in (4, 1, 2, 5):
            landed(p, slot)
        m.stat[p][...] = jnp.ones((128, 128), F32)

        def body(r, carry):
            rows, own, hit = row_span(p, r)
            lt, ls = m.part_t[p][own, :], m.part_s[p][own, :]
            lt = lt + decode(p, 4, rows) + decode(p, 2, rows)
            ls = ls + decode(p, 1, rows) + decode(p, 5, rows)
            m.part_t[p][own, :] = lt
            m.part_s[p][own, :] = ls
            mt = jnp.max(lt, axis=1, keepdims=True)
            ms = jnp.max(ls, axis=1, keepdims=True)
            et = jnp.exp(lt - mt)
            es = jnp.exp(ls - ms)
            values = (
                mt,
                jnp.sum(et, axis=1, keepdims=True),
                jnp.sum(et * (lt - ls), axis=1, keepdims=True),
                ms,
                jnp.sum(es, axis=1, keepdims=True),
                jnp.sum(jnp.where(hit, ls, 0.0), axis=1, keepdims=True),
            )
            lane = iota((16, 128), 1)
            out = jnp.ones((16, 128), F32)
            for i, value in enumerate(values):
                out = jnp.where(lane == i, value, out)
            m.stat[p][rows, :] = out
            return carry

        lax.fori_loop(0, PARTS[p] // 16, body, 0, unroll=True)
        m.stat_z[p][z] = m.stat[p][...].T[0:8, :]
        ref = m.stat_z[p].at[z]
        for k in (4, 3, 5, 2, 6, 1, 7):
            send(ref, ref, m.sz_s[p].at[k], m.sz_r[p].at[z], dev(vocab=lax.rem(z + k, 8)))

    def merge(ref):
        tops_t = [ref[i, 0:1, :] for i in range(8)]
        tops_s = [ref[i, 3:4, :] for i in range(8)]
        mt = functools.reduce(jnp.maximum, tops_t)
        ms = functools.reduce(jnp.maximum, tops_s)
        zt = at = zs = sy = 0.0
        for i in range(8):
            wt_i = jnp.exp(tops_t[i] - mt)
            ws_i = jnp.exp(tops_s[i] - ms)
            zt = zt + ref[i, 1:2, :] * wt_i
            at = at + ref[i, 2:3, :] * wt_i
            zs = zs + ref[i, 4:5, :] * ws_i
            sy = sy + ref[i, 5:6, :]
        return mt, zt, at, ms, zs, sy

    def stats_z(p):
        for k in range(1, 8):
            frm = lax.rem(z + k, 8)
            arrived(m.stat_z[p].at[frm], m.sz_s[p].at[k], m.sz_r[p].at[frm])
        row = iota((8, 128), 0)
        out = jnp.ones((8, 128), F32)
        for i, value in enumerate(merge(m.stat_z[p])):
            out = jnp.where(row == i, value, out)
        m.stat_s[p][s] = out
        ref = m.stat_s[p].at[s]
        for k in (4, 3, 5, 2, 6, 1, 7):
            send(ref, ref, m.ss_s[p].at[k], m.ss_r[p].at[s], dev(section=lax.rem(s + k, 8)))

    losses = []

    def gradient(p):
        n = PARTS[p]
        for k in range(1, 8):
            frm = lax.rem(s + k, 8)
            arrived(m.stat_s[p].at[frm], m.ss_s[p].at[k], m.ss_r[p].at[frm])
        mt, zt, at, ms, zs, sy = merge(m.stat_s[p])
        lse_t = mt + jnp.log(zt)
        lse_s = ms + jnp.log(zs)
        per_token = at / zt - lse_t + lse_s - label_weight * (sy - lse_s)
        per_token = jnp.where(iota((1, 128), 1) < n, per_token, 0.0)
        losses.append(jnp.sum(per_token, axis=1, keepdims=True))
        row = iota((128, 128), 0)
        m.lse[p][...] = jnp.where(row == 0, lse_t, lse_s).T

        def body(r, carry):
            rows, own, hit = row_span(p, r)
            pt = jnp.exp(m.part_t[p][own, :] - m.lse[p][rows, 0:1])
            ps = jnp.exp(m.part_s[p][own, :] - m.lse[p][rows, 1:2])
            value = (1.0 + label_weight) * ps - pt - jnp.where(hit, label_weight, 0.0)
            m.grad[p][own, :] = value.astype(BF16)
            return carry

        lax.fori_loop(0, n // 16, body, 0, unroll=True)
        ref = grad_ref(p, x)
        for k in (2, 1, 3):
            send(ref, ref, m.g_s[p].at[k], m.g_r[p].at[x], dev(dp=lax.rem(x + k, 4)))

    def grad_ref(p, xp):
        n = PARTS[p]
        return m.grad[p].at[pl.ds(pl.multiple_of(xp * n, n), n)]

    def hidden_back(p):
        for k in (1, 3, 2):
            frm = lax.rem(x + k, 4)
            arrived(grad_ref(p, frm), m.g_s[p].at[k], m.g_r[p].at[frm])
        theirs = pl.ds(pl.multiple_of((1 - c) * 256, 256), 256)
        ours = pl.ds(pl.multiple_of(c * 256, 256), 256)
        m.csend[p][...] = mm_nt(m.ws[theirs, :], m.grad[p][...]).astype(BF16)
        send(m.csend[p], m.crecv[p], m.c_s[p], m.c_r[p], other)
        m.hown[p][...] = mm_nt(m.ws[ours, :], m.grad[p][...])

    def slice_ref(ref, zz):
        return ref.at[pl.ds(pl.multiple_of(zz * 32, 32), 32)]

    def hidden_spread(p):
        arrived(m.crecv[p], m.c_s[p], m.c_r[p])
        total = m.hown[p][...] + m.crecv[p][...].astype(F32)
        m.hown[p][...] = total
        m.zsend[p][...] = total.astype(BF16)
        for k in (4, 3, 5, 2, 6, 1, 7):
            to = lax.rem(z + k, 8)
            send(slice_ref(m.zsend[p], to), m.zrecv[p].at[z], m.z_s[p].at[k], m.z_r[p].at[z],
                 dev(vocab=to))

    def hidden_owner(p):
        total = slice_ref(m.hown[p], z)[...]
        for k in range(1, 8):
            frm = lax.rem(z + k, 8)
            arrived(m.zrecv[p].at[frm], m.z_s[p].at[k], m.z_r[p].at[frm])
            total = total + m.zrecv[p][frm].astype(F32)
        m.fsend[p][...] = total.astype(BF16)
        for k in range(4):
            to, here = last_to(k)
            send(m.fsend[p], m.frecv[p].at[y], m.f_s[p].at[k], m.f_r[p].at[y], to,
                 jnp.logical_not(here))

        @pl.when(diagonal)
        def _():
            m.frecv[p][y] = m.fsend[p][...]

    def hidden_final(p):
        n = PARTS[p]
        for k in range(4):
            @pl.when(jnp.logical_not(jnp.logical_and(diagonal, y == k)))
            def _(k=k):
                arrived(m.frecv[p].at[k], m.f_s[p].at[k], m.f_r[p].at[k])
        total = m.frecv[p][0].astype(F32)
        for k in range(1, 4):
            total = total + m.frecv[p][k].astype(F32)
        lane, token = iota((4 * n, tb), 0), iota((4 * n, tb), 1) - starts[p]
        inside = jnp.logical_and(token >= 0, token < n)
        place = ones_where(jnp.logical_and(inside, lane == x * n + token))
        return mm(total.astype(BF16), place)

    def turn_student(p):
        eye = ones_where(iota((128, 128), 0) == iota((128, 128), 1))
        for u in range(4):
            lanes = slice(512 + (u % 2) * 128, 640 + (u % 2) * 128)
            flat = mm_nt(eye, m.hid[p][u // 2, :, lanes])
            m.hst[p][u * 128:(u + 1) * 128, :] = flat.astype(BF16)

    def head_terms():
        def body(i, carry):
            cols = pl.ds(pl.multiple_of(i * 256, 256), 256)
            total = None
            for p in range(len(PARTS)):
                term = mm(m.hst[p][...], m.grad[p][:, cols])
                total = term if total is None else total + term
            hg[:, cols] = total
            return carry
        lax.fori_loop(0, vb // 256, body, 0)

    def prepare():
        m.wide[...] = jnp.zeros_like(m.wide)
        m.wide[0:1, 0:tb] = m.lab[...].astype(F32)
        m.lab_col[...] = m.wide[...].T
        for k in range(4):
            rows, lanes = iota((128, 384), 0), iota((128, 384), 1)
            place = jnp.where(rows < 64, rows + 64 * k, rows - 64 + 256 + 32 * k)
            picks.append(ones_where(jnp.logical_and(lanes == place, rows < 96)))
        local[3].wait()
        local[4].wait()

    def loss_send():
        m.loss[x] = jnp.broadcast_to(functools.reduce(jnp.add, losses), (8, 128))
        for k in range(1, 4):
            send(m.loss.at[x], m.loss.at[x], m.l_s.at[k], m.l_r.at[x], dev(dp=lax.rem(x + k, 4)))

    def loss_sum():
        for k in range(1, 4):
            frm = lax.rem(x + k, 4)
            arrived(m.loss.at[frm], m.l_s.at[k], m.l_r.at[frm])
        loss = functools.reduce(jnp.add, [m.loss[k, 0:1, 0:1] for k in range(4)])
        loss_out[0, 0] = jnp.sum(loss) / (4.0 * tb)

    def finish():
        for cond, copy in pending:
            if cond is None:
                copy.wait_send()
            else:
                pl.when(cond)(copy.wait_send)
        out = functools.reduce(jnp.add, [hidden_final(p) for p in range(len(PARTS))])
        hid_out[...] = out.astype(BF16)

    per_part = {
        "F": hidden_first, "Z": hidden_z, "Y": hidden_y, "W": hidden_swap, "L": logits,
        "U": turn_student, "O": fold, "T": total_logits, "S": stats_z, "G": gradient,
        "B": hidden_back, "P": hidden_spread, "N": hidden_owner,
    }
    once = {"I": prepare, "X": loss_send, "X2": loss_sum, "H": head_terms, "E": finish}
    for step in ORDER:
        if step in once:
            once[step]()
        else:
            per_part[step[0]](int(step[1]))


def per_device(teacher_hidden, student_hidden, teacher_head, student_head, labels):
    tb = teacher_hidden.shape[0]
    kt, vb = teacher_head.shape
    ks = student_head.shape[0]
    spec = buffers(tb, kt, ks, vb)
    flat = []
    for shape in spec.values():
        flat.extend(shape if isinstance(shape, list) else [shape])
    hbm = pl.BlockSpec(memory_space=pltpu.HBM)
    vmem = pl.BlockSpec(memory_space=pltpu.VMEM)
    loss, head_grad, hidden_grad = pl.pallas_call(
        functools.partial(kernel, spec),
        out_shape=(
            jax.ShapeDtypeStruct((1, 1), F32),
            pltpu.VMEM((ks, vb), F32),
            pltpu.VMEM((32, tb), BF16),
        ),
        in_specs=[hbm] * 5,
        out_specs=(pl.BlockSpec(memory_space=pltpu.SMEM), vmem, vmem),
        scratch_shapes=flat,
        compiler_params=pltpu.CompilerParams(
            collective_id=0, has_side_effects=True, vmem_limit_bytes=58 * 1024 * 1024
        ),
    )(teacher_hidden.T, student_hidden.T, teacher_head, student_head, labels.reshape(1, tb))
    return (loss.reshape(()), head_grad, hidden_grad.T)


def solution(mesh):
    spec = P("dp", ("section", "vocab"))
    return jax.shard_map(
        per_device,
        mesh=mesh,
        in_specs=(spec, spec, spec, spec, P("dp")),
        out_specs=(P(), spec, spec),
        check_vma=False,
    )
```

```python
import functools
import jax
import jax.numpy as jnp
from jax import lax
from jax.experimental import pallas as pl
from jax.experimental.pallas import tpu as pltpu
from jax.sharding import PartitionSpec as P

label_weight = 0.5
MESH = pl.DeviceIdType.MESH
F32, BF16, I32, I16 = jnp.float32, jnp.bfloat16, jnp.int32, jnp.int16
TOP = 14.99
PARTS = (48, 64, 48)
ORDER = (
    "F", "I", "Z2", "Z1", "Y2", "Y1", "W2", "Z0", "L2", "W1", "Y0", "U2",
    "O2", "L1", "T2", "W0", "O1", "L0", "U1", "T1", "S2", "O0", "S1", "G2", "T0", "G1",
    "U0", "S0", "B2", "G0", "P2", "B1", "P1", "B0", "P0", "N1", "X", "N2", "H", "X2",
    "N0", "E",
)


def mm(a, b):
    return jnp.dot(a, b, preferred_element_type=F32)


def mm_nt(a, b):
    return lax.dot_general(a, b, (((1,), (1,)), ((), ())), preferred_element_type=F32)


def iota(shape, dim):
    return lax.broadcasted_iota(I32, shape, dim)


def ones_where(mask):
    return jnp.where(mask, 1.0, 0.0).astype(BF16)


def buffers(tb, kt, ks, vb):
    dma, vmem = pltpu.SemaphoreType.DMA, pltpu.VMEM

    def each(make):
        return [make(n) for n in PARTS]

    return {
        "wt": vmem((kt, vb), BF16),
        "ws": vmem((ks, vb), BF16),
        "lab": vmem((1, tb), I32),
        "turned": vmem((128, tb), BF16),
        "packed": vmem((tb, 128), BF16),
        "wide": vmem((128, 256), F32),
        "lab_col": vmem((256, 128), F32),
        "raw": vmem((8, tb, 128), BF16),
        "hid": each(lambda n: vmem((2, 4 * n, 768), BF16)),
        "hst": each(lambda n: vmem((ks, 4 * n), BF16)),
        "part_t": each(lambda n: vmem((4 * n, vb), F32)),
        "part_s": each(lambda n: vmem((4 * n, vb), F32)),
        "qsend": each(lambda n: vmem((6, n, vb + 128), I16)),
        "qrecv": each(lambda n: vmem((6, n, vb + 128), I16)),
        "level": each(lambda n: vmem((2, n, 128), F32)),
        "stat": each(lambda n: vmem((128, 128), F32)),
        "lse": each(lambda n: vmem((128, 128), F32)),
        "stat_z": each(lambda n: vmem((8, 8, 128), F32)),
        "stat_s": each(lambda n: vmem((8, 8, 128), F32)),
        "grad": each(lambda n: vmem((4 * n, vb), BF16)),
        "hown": each(lambda n: vmem((256, 4 * n), F32)),
        "csend": each(lambda n: vmem((256, 4 * n), BF16)),
        "crecv": each(lambda n: vmem((256, 4 * n), BF16)),
        "zsend": each(lambda n: vmem((256, 4 * n), BF16)),
        "zrecv": each(lambda n: vmem((8, 32, 4 * n), BF16)),
        "fsend": each(lambda n: vmem((32, 4 * n), BF16)),
        "frecv": each(lambda n: vmem((4, 32, 4 * n), BF16)),
        "loss": vmem((4, 8, 128), F32),
        "in_sem": dma((5,)),
        "h_s": dma,
        "h_r": dma,
        "r_s": each(lambda n: dma((8,))),
        "r_r": each(lambda n: dma((8,))),
        "u_s": each(lambda n: dma((4,))),
        "u_r": each(lambda n: dma((4,))),
        "w_s": each(lambda n: dma((4,))),
        "w_r": each(lambda n: dma((4,))),
        "q_s": each(lambda n: dma((6,))),
        "q_r": each(lambda n: dma((6,))),
        "sz_s": each(lambda n: dma((8,))),
        "sz_r": each(lambda n: dma((8,))),
        "ss_s": each(lambda n: dma((8,))),
        "ss_r": each(lambda n: dma((8,))),
        "g_s": each(lambda n: dma((4,))),
        "g_r": each(lambda n: dma((4,))),
        "c_s": each(lambda n: dma),
        "c_r": each(lambda n: dma),
        "z_s": each(lambda n: dma((8,))),
        "z_r": each(lambda n: dma((8,))),
        "f_s": each(lambda n: dma((4,))),
        "f_r": each(lambda n: dma((4,))),
        "l_s": dma((4,)),
        "l_r": dma((4,)),
    }


class Refs:
    pass


def kernel(spec, th, sh, wt_hbm, ws_hbm, lab_hbm, loss_out, hg, hid_out, *scratch):
    m = Refs()
    scratch = list(scratch)
    for name, shape in spec.items():
        if isinstance(shape, list):
            setattr(m, name, [scratch.pop(0) for _ in shape])
        else:
            setattr(m, name, scratch.pop(0))
    tb = m.packed.shape[0]
    vb = m.wt.shape[1]
    s = lax.axis_index("section")
    z = lax.axis_index("vocab")
    x = lax.axis_index("dp")
    y, c = lax.div(s, 2), lax.rem(s, 2)
    right, left, opp = lax.rem(x + 1, 4), lax.rem(x + 3, 4), lax.rem(x + 2, 4)
    diagonal = x == y
    crossed = jnp.logical_not(diagonal)
    offset = (s * 8 + z) * vb
    starts = [sum(PARTS[:k]) for k in range(len(PARTS))]
    pending, steps = [], []

    def dev(section=s, vocab=z, dp=x):
        return {"section": section, "vocab": vocab, "dp": dp}

    def remote(src, dst, ssem, rsem, to):
        return pltpu.make_async_remote_copy(
            src_ref=src, dst_ref=dst, send_sem=ssem, recv_sem=rsem,
            device_id=to, device_id_type=MESH,
        )

    def send(src, dst, ssem, rsem, to, cond=None):
        copy = remote(src, dst, ssem, rsem, to)
        if cond is None:
            copy.start()
        else:
            pl.when(cond)(copy.start)
        pending.append((len(steps), cond, copy))

    def arrived(dst, ssem, rsem):
        remote(dst, dst, ssem, rsem, dev(dp=right)).wait_recv()

    other = dev(section=s + 1 - 2 * c)

    local = [
        pltpu.make_async_copy(th, m.turned.at[0:64], m.in_sem.at[0]),
        pltpu.make_async_copy(sh, m.turned.at[64:96], m.in_sem.at[1]),
        pltpu.make_async_copy(lab_hbm, m.lab, m.in_sem.at[2]),
        pltpu.make_async_copy(wt_hbm, m.wt, m.in_sem.at[3]),
        pltpu.make_async_copy(ws_hbm, m.ws, m.in_sem.at[4]),
    ]
    for copy in local:
        copy.start()

    barrier = pltpu.get_barrier_semaphore()

    def greet(to, unless=None):
        signal = functools.partial(
            pl.semaphore_signal, barrier, inc=1, device_id=to, device_id_type=MESH
        )
        if unless is None:
            signal()
        else:
            pl.when(jnp.logical_not(unless))(signal)

    def last_to(k):
        return dev(section=2 * x + c, dp=k), jnp.logical_and(diagonal, x == k)

    for k in range(1, 8):
        greet(dev(vocab=lax.rem(z + k, 8)))
    for k in range(1, 4):
        greet(dev(section=2 * x + c, dp=lax.rem(x + k, 4)))
    for k in range(4):
        greet(dev(section=2 * k + c, dp=y), diagonal)
    for k in range(1, 4):
        greet(dev(dp=lax.rem(x + k, 4)))
    for k in range(1, 8):
        greet(dev(section=lax.rem(s + k, 8)))

    for copy in local[:3]:
        copy.wait()
    m.turned[96:128, :] = jnp.zeros((32, tb), BF16)
    m.packed[...] = mm_nt(
        ones_where(iota((tb, tb), 0) == iota((tb, tb), 1)), m.turned[...]
    ).astype(BF16)
    pl.semaphore_wait(barrier, 20 + 4 * crossed.astype(I32))

    def hidden_first():
        send(m.packed, m.raw.at[z], m.h_s, m.h_r, dev(section=2 * x + c, dp=y), crossed)

        @pl.when(diagonal)
        def _():
            m.raw[z] = m.packed[...]

    def raw_ref(p, zz):
        return m.raw.at[zz, pl.ds(starts[p], PARTS[p])]

    def hidden_z(p):
        if not any(step[0] == "Z" for step in steps[:-1]):
            @pl.when(crossed)
            def _():
                arrived(m.raw.at[z], m.h_s, m.h_r)

        ref = raw_ref(p, z)
        for k in (4, 3, 5, 2, 6, 1, 7):
            send(ref, ref, m.r_s[p].at[k], m.r_r[p].at[z], dev(vocab=lax.rem(z + k, 8)))

    picks = []

    def hid_ref(p, core, yy):
        n = PARTS[p]
        return m.hid[p].at[core, pl.ds(pl.multiple_of(yy * n, n), n)]

    def hidden_y(p):
        for k in (1, 7, 2, 6, 3, 5, 4):
            frm = lax.rem(z + k, 8)
            arrived(raw_ref(p, frm), m.r_s[p].at[k], m.r_r[p].at[frm])
        ref = hid_ref(p, c, y)
        for g in range(2):
            total = None
            for k in range(4):
                term = mm(raw_ref(p, 4 * g + k)[...], picks[k])
                total = term if total is None else total + term
            ref[:, g * 256:(g + 1) * 256] = total[:, 0:256].astype(BF16)
            ref[:, 512 + g * 128:512 + (g + 1) * 128] = total[:, 256:384].astype(BF16)
        for k in (2, 1, 3):
            to = lax.rem(y + k, 4)
            send(ref, ref, m.u_s[p].at[k], m.u_r[p].at[y], dev(section=2 * to + c))
        send(ref, ref, m.w_s[p].at[y], m.w_r[p].at[y], other)

    def hidden_swap(p):
        for k in (1, 3, 2):
            frm = lax.rem(y + k, 4)
            ref = hid_ref(p, c, frm)
            arrived(ref, m.u_s[p].at[k], m.u_r[p].at[frm])
            send(ref, ref, m.w_s[p].at[frm], m.w_r[p].at[frm], other)

    def decode(p, slot, rows):
        if slot in (1, 4):
            level = m.qrecv[p][slot + 1, rows, vb:vb + 128][:, 64:65]
        else:
            level = m.qrecv[p][slot, rows, vb:vb + 128][:, 0:1]
        step = jnp.exp2(jnp.broadcast_to(level.astype(F32), (16, 128)) * 0.25 - TOP)
        return jnp.concatenate(
            [m.qrecv[p][slot, rows, i:i + 128].astype(F32) * step for i in range(0, vb, 128)],
            axis=1,
        )

    def word_refs(p, slot):
        lanes = slice(0, vb if slot in (1, 4) else vb + 128)
        return m.qsend[p].at[slot, :, lanes], m.qrecv[p].at[slot, :, lanes]

    def encode(p, slot, src, xp, dp, add=None):
        n = PARTS[p]

        def body(r, carry):
            rows = pl.ds(pl.multiple_of(r * 16, 16), 16)
            v = src[pl.ds(pl.multiple_of(xp * n + r * 16, 16), 16), :]
            if add is not None:
                v = v + decode(p, add, rows)
            top = jnp.maximum(jnp.max(jnp.abs(v), axis=1, keepdims=True), 1e-30)
            level = jnp.broadcast_to(jnp.ceil(jnp.log2(top) * 4.0), (16, 128))
            scale = jnp.exp2(TOP - level * 0.25)
            for i in range(0, vb, 128):
                q = jnp.round(v[:, i:i + 128] * scale).astype(I32)
                m.qsend[p][slot, rows, i:i + 128] = q.astype(I16)
            if slot in (1, 4):
                m.level[p][slot // 4, rows, :] = level
            else:
                if slot in (2, 5):
                    beside = m.level[p][slot // 5, rows, :]
                    level = jnp.where(iota((16, 128), 1) < 64, level, beside)
                m.qsend[p][slot, rows, vb:vb + 128] = level.astype(I32).astype(I16)
            return carry

        lax.fori_loop(0, n // 16, body, 0, unroll=True)
        src_words, dst_words = word_refs(p, slot)
        send(src_words, dst_words, m.q_s[p].at[slot], m.q_r[p].at[slot], dev(dp=dp))

    def landed(p, slot):
        arrived(word_refs(p, slot)[1], m.q_s[p].at[slot], m.q_r[p].at[slot])

    def logits(p):
        for k in range(4):
            arrived(hid_ref(p, 1 - c, k), m.w_s[p].at[k], m.w_r[p].at[k])

        def product(out, weights, lanes, depth):
            def body(i, carry):
                cols = pl.ds(pl.multiple_of(i * 256, 256), 256)
                out[:, cols] = mm(m.hid[p][0, :, lanes], weights[0:depth, cols]) + mm(
                    m.hid[p][1, :, lanes], weights[depth:2 * depth, cols]
                )
                return carry
            lax.fori_loop(0, vb // 256, body, 0)

        product(m.part_t[p], m.wt, slice(0, 512), 512)
        encode(p, 0, m.part_t[p], opp, right)
        product(m.part_s[p], m.ws, slice(512, 768), 256)
        encode(p, 3, m.part_s[p], opp, left)
        encode(p, 1, m.part_s[p], right, right)
        encode(p, 4, m.part_t[p], left, left)

    def fold(p):
        landed(p, 0)
        encode(p, 2, m.part_t[p], right, right, add=0)
        landed(p, 3)
        encode(p, 5, m.part_s[p], left, left, add=3)

    def row_span(p, r):
        n = PARTS[p]
        rows = pl.ds(pl.multiple_of(r * 16, 16), 16)
        own = pl.ds(pl.multiple_of(x * n + r * 16, 16), 16)
        toks = pl.ds(pl.multiple_of(starts[p] + r * 16, 16), 16)
        hit = offset + iota((16, vb), 1) == m.lab_col[toks, 0:1].astype(I32)
        return rows, own, hit

    def total_logits(p):
        for slot in (4, 1, 2, 5):
            landed(p, slot)
        m.stat[p][...] = jnp.ones((128, 128), F32)

        def body(r, carry):
            rows, own, hit = row_span(p, r)
            lt, ls = m.part_t[p][own, :], m.part_s[p][own, :]
            lt = lt + decode(p, 4, rows) + decode(p, 2, rows)
            ls = ls + decode(p, 1, rows) + decode(p, 5, rows)
            m.part_t[p][own, :] = lt
            m.part_s[p][own, :] = ls
            mt = jnp.max(lt, axis=1, keepdims=True)
            ms = jnp.max(ls, axis=1, keepdims=True)
            et = jnp.exp(lt - mt)
            es = jnp.exp(ls - ms)
            values = (
                mt,
                jnp.sum(et, axis=1, keepdims=True),
                jnp.sum(et * (lt - ls), axis=1, keepdims=True),
                ms,
                jnp.sum(es, axis=1, keepdims=True),
                jnp.sum(jnp.where(hit, ls, 0.0), axis=1, keepdims=True),
            )
            lane = iota((16, 128), 1)
            out = jnp.ones((16, 128), F32)
            for i, value in enumerate(values):
                out = jnp.where(lane == i, value, out)
            m.stat[p][rows, :] = out
            return carry

        lax.fori_loop(0, PARTS[p] // 16, body, 0, unroll=True)
        m.stat_z[p][z] = m.stat[p][...].T[0:8, :]
        ref = m.stat_z[p].at[z]
        for k in (4, 3, 5, 2, 6, 1, 7):
            send(ref, ref, m.sz_s[p].at[k], m.sz_r[p].at[z], dev(vocab=lax.rem(z + k, 8)))

    def merge(ref):
        tops_t = [ref[i, 0:1, :] for i in range(8)]
        tops_s = [ref[i, 3:4, :] for i in range(8)]
        mt = functools.reduce(jnp.maximum, tops_t)
        ms = functools.reduce(jnp.maximum, tops_s)
        zt = at = zs = sy = 0.0
        for i in range(8):
            wt_i = jnp.exp(tops_t[i] - mt)
            ws_i = jnp.exp(tops_s[i] - ms)
            zt = zt + ref[i, 1:2, :] * wt_i
            at = at + ref[i, 2:3, :] * wt_i
            zs = zs + ref[i, 4:5, :] * ws_i
            sy = sy + ref[i, 5:6, :]
        return mt, zt, at, ms, zs, sy

    def stats_z(p):
        for k in range(1, 8):
            frm = lax.rem(z + k, 8)
            arrived(m.stat_z[p].at[frm], m.sz_s[p].at[k], m.sz_r[p].at[frm])
        row = iota((8, 128), 0)
        out = jnp.ones((8, 128), F32)
        for i, value in enumerate(merge(m.stat_z[p])):
            out = jnp.where(row == i, value, out)
        m.stat_s[p][s] = out
        ref = m.stat_s[p].at[s]
        for k in (4, 3, 5, 2, 6, 1, 7):
            send(ref, ref, m.ss_s[p].at[k], m.ss_r[p].at[s], dev(section=lax.rem(s + k, 8)))

    losses = []

    def gradient(p):
        n = PARTS[p]
        for k in range(1, 8):
            frm = lax.rem(s + k, 8)
            arrived(m.stat_s[p].at[frm], m.ss_s[p].at[k], m.ss_r[p].at[frm])
        mt, zt, at, ms, zs, sy = merge(m.stat_s[p])
        lse_t = mt + jnp.log(zt)
        lse_s = ms + jnp.log(zs)
        per_token = at / zt - lse_t + lse_s - label_weight * (sy - lse_s)
        per_token = jnp.where(iota((1, 128), 1) < n, per_token, 0.0)
        losses.append(jnp.sum(per_token, axis=1, keepdims=True))
        row = iota((128, 128), 0)
        m.lse[p][...] = jnp.where(row == 0, lse_t, lse_s).T

        def body(r, carry):
            rows, own, hit = row_span(p, r)
            pt = jnp.exp(m.part_t[p][own, :] - m.lse[p][rows, 0:1])
            ps = jnp.exp(m.part_s[p][own, :] - m.lse[p][rows, 1:2])
            value = (1.0 + label_weight) * ps - pt - jnp.where(hit, label_weight, 0.0)
            m.grad[p][own, :] = value.astype(BF16)
            return carry

        lax.fori_loop(0, n // 16, body, 0, unroll=True)
        ref = grad_ref(p, x)
        for k in (2, 1, 3):
            send(ref, ref, m.g_s[p].at[k], m.g_r[p].at[x], dev(dp=lax.rem(x + k, 4)))

    def grad_ref(p, xp):
        n = PARTS[p]
        return m.grad[p].at[pl.ds(pl.multiple_of(xp * n, n), n)]

    def hidden_back(p):
        for k in (1, 3, 2):
            frm = lax.rem(x + k, 4)
            arrived(grad_ref(p, frm), m.g_s[p].at[k], m.g_r[p].at[frm])
        theirs = pl.ds(pl.multiple_of((1 - c) * 256, 256), 256)
        ours = pl.ds(pl.multiple_of(c * 256, 256), 256)
        m.csend[p][...] = mm_nt(m.ws[theirs, :], m.grad[p][...]).astype(BF16)
        send(m.csend[p], m.crecv[p], m.c_s[p], m.c_r[p], other)
        m.hown[p][...] = mm_nt(m.ws[ours, :], m.grad[p][...])

    def slice_ref(ref, zz):
        return ref.at[pl.ds(pl.multiple_of(zz * 32, 32), 32)]

    def hidden_spread(p):
        arrived(m.crecv[p], m.c_s[p], m.c_r[p])
        total = m.hown[p][...] + m.crecv[p][...].astype(F32)
        m.hown[p][...] = total
        m.zsend[p][...] = total.astype(BF16)
        for k in (4, 3, 5, 2, 6, 1, 7):
            to = lax.rem(z + k, 8)
            send(slice_ref(m.zsend[p], to), m.zrecv[p].at[z], m.z_s[p].at[k], m.z_r[p].at[z],
                 dev(vocab=to))

    def hidden_owner(p):
        total = slice_ref(m.hown[p], z)[...]
        for k in range(1, 8):
            frm = lax.rem(z + k, 8)
            arrived(m.zrecv[p].at[frm], m.z_s[p].at[k], m.z_r[p].at[frm])
            total = total + m.zrecv[p][frm].astype(F32)
        m.fsend[p][...] = total.astype(BF16)
        for k in range(4):
            to, here = last_to(k)
            send(m.fsend[p], m.frecv[p].at[y], m.f_s[p].at[k], m.f_r[p].at[y], to,
                 jnp.logical_not(here))

        @pl.when(diagonal)
        def _():
            m.frecv[p][y] = m.fsend[p][...]

    def hidden_final(p):
        n = PARTS[p]
        for k in range(4):
            @pl.when(jnp.logical_not(jnp.logical_and(diagonal, y == k)))
            def _(k=k):
                arrived(m.frecv[p].at[k], m.f_s[p].at[k], m.f_r[p].at[k])
        total = m.frecv[p][0].astype(F32)
        for k in range(1, 4):
            total = total + m.frecv[p][k].astype(F32)
        lane, token = iota((4 * n, tb), 0), iota((4 * n, tb), 1) - starts[p]
        inside = jnp.logical_and(token >= 0, token < n)
        place = ones_where(jnp.logical_and(inside, lane == x * n + token))
        return mm(total.astype(BF16), place)

    def turn_student(p):
        eye = ones_where(iota((128, 128), 0) == iota((128, 128), 1))
        for u in range(4):
            lanes = slice(512 + (u % 2) * 128, 640 + (u % 2) * 128)
            flat = mm_nt(eye, m.hid[p][u // 2, :, lanes])
            m.hst[p][u * 128:(u + 1) * 128, :] = flat.astype(BF16)

    def head_terms():
        def body(i, carry):
            cols = pl.ds(pl.multiple_of(i * 256, 256), 256)
            total = None
            for p in range(len(PARTS)):
                term = mm(m.hst[p][...], m.grad[p][:, cols])
                total = term if total is None else total + term
            hg[:, cols] = total
            return carry
        lax.fori_loop(0, vb // 256, body, 0)

    def prepare():
        m.wide[...] = jnp.zeros_like(m.wide)
        m.wide[0:1, 0:tb] = m.lab[...].astype(F32)
        m.lab_col[...] = m.wide[...].T
        for k in range(4):
            rows, lanes = iota((128, 384), 0), iota((128, 384), 1)
            place = jnp.where(rows < 64, rows + 64 * k, rows - 64 + 256 + 32 * k)
            picks.append(ones_where(jnp.logical_and(lanes == place, rows < 96)))
        local[3].wait()
        local[4].wait()

    def loss_send():
        m.loss[x] = jnp.broadcast_to(functools.reduce(jnp.add, losses), (8, 128))
        for k in range(1, 4):
            send(m.loss.at[x], m.loss.at[x], m.l_s.at[k], m.l_r.at[x], dev(dp=lax.rem(x + k, 4)))

    def loss_sum():
        for k in range(1, 4):
            frm = lax.rem(x + k, 4)
            arrived(m.loss.at[frm], m.l_s.at[k], m.l_r.at[frm])
        loss = functools.reduce(jnp.add, [m.loss[k, 0:1, 0:1] for k in range(4)])
        loss_out[0, 0] = jnp.sum(loss) / (4.0 * tb)

    def settle(age):
        while pending and len(steps) - pending[0][0] >= age:
            _, cond, copy = pending.pop(0)
            if cond is None:
                copy.wait_send()
            else:
                pl.when(cond)(copy.wait_send)

    def finish():
        settle(0)
        out = functools.reduce(jnp.add, [hidden_final(p) for p in range(len(PARTS))])
        hid_out[...] = out.astype(BF16)

    per_part = {
        "Z": hidden_z, "Y": hidden_y, "W": hidden_swap, "L": logits,
        "U": turn_student, "O": fold, "T": total_logits, "S": stats_z, "G": gradient,
        "B": hidden_back, "P": hidden_spread, "N": hidden_owner,
    }
    once = {"F": hidden_first, "I": prepare, "X": loss_send, "X2": loss_sum, "H": head_terms, "E": finish}
    for step in ORDER:
        steps.append(step)
        if step[0] in "SGBN":
            settle(8)
        if step in once:
            once[step]()
        else:
            per_part[step[0]](int(step[1]))


def per_device(teacher_hidden, student_hidden, teacher_head, student_head, labels):
    tb = teacher_hidden.shape[0]
    kt, vb = teacher_head.shape
    ks = student_head.shape[0]
    spec = buffers(tb, kt, ks, vb)
    flat = []
    for shape in spec.values():
        flat.extend(shape if isinstance(shape, list) else [shape])
    hbm = pl.BlockSpec(memory_space=pltpu.HBM)
    vmem = pl.BlockSpec(memory_space=pltpu.VMEM)
    loss, head_grad, hidden_grad = pl.pallas_call(
        functools.partial(kernel, spec),
        out_shape=(
            jax.ShapeDtypeStruct((1, 1), F32),
            pltpu.VMEM((ks, vb), F32),
            pltpu.VMEM((32, tb), BF16),
        ),
        in_specs=[hbm] * 5,
        out_specs=(pl.BlockSpec(memory_space=pltpu.SMEM), vmem, vmem),
        scratch_shapes=flat,
        compiler_params=pltpu.CompilerParams(
            collective_id=0, has_side_effects=True, vmem_limit_bytes=58 * 1024 * 1024
        ),
    )(teacher_hidden.T, student_hidden.T, teacher_head, student_head, labels.reshape(1, tb))
    return (loss.reshape(()), head_grad, hidden_grad.T)


def solution(mesh):
    spec = P("dp", ("section", "vocab"))
    return jax.shard_map(
        per_device,
        mesh=mesh,
        in_specs=(spec, spec, spec, spec, P("dp")),
        out_specs=(P(), spec, spec),
        check_vma=False,
    )
```
